32 devices in a mesh: frame: 8 (over z, y), coord: 4 (over x, core).
Axes of the slice: x: 2, y: 2, z: 4, core: 2. Of those that a mesh axis runs over, the one named last changes fastest.
Arguments:
- frames: bfloat16 [8192, 4224], P('frame'), may hold values from -0.5 to 1.5
- b_values: bfloat16 [4096, 512], P('coord'), may hold values from -0.25 to 0.25
- b_cols: int32 [64, 8], P('coord'), may hold values from 0 to 65, as said below
- frame_window: int32 [8192], P('frame'), may hold values from 0 to 1, as said below
Outputs:
- count: float32 [], replicated
- mean: float32 [4096], P('coord')
- covariance: float32 [4096, 4096], P('frame', 'coord')
The draws below stay inside these ranges and needn't reach their ends.
Inputs may be any that keep to these rules, and one draw needn't show every extreme that they name: `b_cols`: each row holds 8 different column-block indices. `frame_window`: the first and the last frame are always in the window.
All inputs are finite; a program needn't handle non-finite values.
Results may differ from the reference program's by a relative error of at most 0.0022.
Values may be sent and summed in bfloat16 or wider, within the bound.
No kernel may reach another device: no remote copies, remote signals or barrier semaphores. Data moves between devices by JAX's collectives and lax.ppermute only.
A program may use at most 128 MiB of HBM per device.

```python
import jax
import jax.numpy as jnp
from jax import lax

CART = 4224
NQ = 4096
BLOCK = 64
KB = 8
FRAMES = 8192
CB = 66
NQB = 64


def draw_b_cols(key, part):
    row_keys = jax.random.split(key, NQB)
    chosen = jax.vmap(lambda row_key: jax.random.permutation(row_key, CB)[:KB])(row_keys)
    return chosen.astype(jnp.int32)


def draw_frame_window(key, part):
    index = jnp.arange(FRAMES, dtype=jnp.int32)
    rolls = jax.random.randint(key, (FRAMES,), 0, 4 * FRAMES, dtype=jnp.int32)
    inside = (rolls < FRAMES + 2 * index) | (index == 0) | (index == FRAMES - 1)
    return inside.astype(jnp.int32)


def steps_of(own_key, extent, pieces, low, top_value):
    factor_of = 1.0
    for dim, blocks in pieces:
        heights = jax.random.uniform(jax.random.fold_in(jax.random.fold_in(own_key, 6), dim), (blocks,), jnp.float32, low / len(pieces), top_value / len(pieces))
        factor_of = factor_of * jnp.repeat(jnp.exp(heights), extent[dim] // blocks).reshape((-1,) + (1,) * (len(extent) - 1 - dim))
    return factor_of


def noise(own_key, shape, scale, bound, shards=(), kind=jnp.bfloat16):
    drawn = scale * jax.random.normal(own_key, shape, jnp.float32)
    if shards:
        drawn = drawn * steps_of(own_key, shape, shards, -0.22, 0.18)
    return jnp.clip(drawn, -bound, bound).astype(kind)


def setup_inputs(seed: int = 0) -> dict:
    streams_of = jax.random.split(jax.random.key(seed), 5)
    frames = jnp.clip(-0.5 + 2.0 * jax.random.uniform(streams_of[0], (FRAMES, CART), jnp.float32) ** steps_of(streams_of[0], (FRAMES, CART), ((0, 8),), -0.2, 0.2), -0.5, 1.5).astype(jnp.bfloat16)
    b_values = noise(streams_of[1], (NQ, KB * BLOCK), (KB * BLOCK) ** -0.5, 0.25, ((0, 4),))
    b_cols = draw_b_cols(jax.random.fold_in(streams_of[4], 71), 0)
    frame_window = draw_frame_window(jax.random.fold_in(streams_of[4], 71), 0)
    return {"frames": frames, "b_values": b_values, "b_cols": b_cols, "frame_window": frame_window}


def reference(frames, b_values, b_cols, frame_window):
    blocks = frames.reshape(FRAMES, CB, BLOCK)

    def one_block(row_block):
        picked = jnp.take(blocks, b_cols[row_block], axis=1).reshape(FRAMES, KB * BLOCK)
        rows_here = lax.dynamic_slice_in_dim(b_values, (row_block * BLOCK).astype(jnp.int32), BLOCK, 0)
        product = lax.dot_general(picked, rows_here, (((1,), (1,)), ((), ())), preferred_element_type=jnp.float32)
        return product.astype(jnp.bfloat16)

    coords_q = lax.map(one_block, jnp.arange(NQB, dtype=jnp.int32))
    coords_q = jnp.transpose(coords_q, (1, 0, 2)).reshape(FRAMES, NQ)
    weight = frame_window.astype(jnp.float32)
    count = jnp.sum(weight)
    coords_f = coords_q.astype(jnp.float32)
    mean = jnp.dot(weight, coords_f, precision=lax.Precision.HIGHEST) / count
    centered = (weight[:, None] * (coords_f - mean)).astype(jnp.bfloat16)
    centered_f = centered.astype(jnp.float32)
    covariance = jnp.dot(centered_f.T, centered_f, precision=lax.Precision.HIGHEST) / (count - 1.0)
    return count, mean, covariance
```

```python
import jax
import jax.numpy as jnp
from jax import lax
from jax.experimental import pallas as pl
from jax.experimental.pallas import tpu as pltpu
from jax.sharding import PartitionSpec as P

BLOCK = 64
CHUNKS = 4
F32, F16, BF16 = jnp.float32, jnp.float16, jnp.bfloat16


def project_kernel(cols_ref, frames_ref, values_ref, weight_ref, out_ref, sums_ref, dense_ref):
    row_blocks, nonzero = cols_ref.shape

    @pl.when(pl.program_id(0) == 0)
    def _():
        dense_ref[...] = jnp.zeros_like(dense_ref)
        sums_ref[...] = jnp.zeros_like(sums_ref)
        for r in range(row_blocks):
            block = values_ref[r * BLOCK : (r + 1) * BLOCK, :].astype(F32).T.astype(BF16)
            for k in range(nonzero):
                start = pl.multiple_of(cols_ref[r, k] * BLOCK, BLOCK)
                dense_ref[pl.ds(start, BLOCK), r * BLOCK : (r + 1) * BLOCK] = block[
                    k * BLOCK : (k + 1) * BLOCK, :
                ]

    product = jnp.dot(frames_ref[...], dense_ref[...], preferred_element_type=F32)
    coords = product.astype(BF16).astype(F32)
    out_ref[...] = coords.T.astype(BF16)
    weighted = coords * weight_ref[...]
    sums_ref[0:1, :] += jnp.sum(weighted, axis=0, keepdims=True)
    sums_ref[1:2, :] += jnp.sum(weighted * coords, axis=0, keepdims=True)


def project(frames, values, cols, weight):
    rows, cart = frames.shape
    width = values.shape[0]
    tile = min(256, rows)
    return pl.pallas_call(
        project_kernel,
        grid=(rows // tile,),
        in_specs=[
            pl.BlockSpec(memory_space=pltpu.SMEM),
            pl.BlockSpec((tile, cart), lambda i: (i, 0)),
            pl.BlockSpec(values.shape, lambda i: (0, 0)),
            pl.BlockSpec((tile, 1), lambda i: (i, 0)),
        ],
        out_specs=[
            pl.BlockSpec((width, tile), lambda i: (0, i)),
            pl.BlockSpec((8, width), lambda i: (0, 0)),
        ],
        out_shape=[
            jax.ShapeDtypeStruct((width, rows), BF16),
            jax.ShapeDtypeStruct((8, width), F32),
        ],
        scratch_shapes=[pltpu.VMEM((cart, width), BF16)],
        compiler_params=pltpu.CompilerParams(vmem_limit_bytes=48 * 2**20),
        cost_estimate=pl.CostEstimate(
            flops=2 * rows * cart * width, bytes_accessed=2 * rows * (cart + width), transcendentals=0
        ),
        name="project",
    )(cols, frames, values, weight[:, None])


def solution(mesh):
    n_f, n_c = mesh.shape["frame"], mesh.shape["coord"]
    m = n_f // n_c
    low = m.bit_length() - 1
    high = n_c.bit_length() - 1

    def swap(x, axis, bit):
        size = mesh.shape[axis]
        return lax.ppermute(x, axis, [(i, i ^ bit) for i in range(size)])

    def on_device(frames, b_values, b_cols, frame_window):
        f, c = lax.axis_index("frame"), lax.axis_index("coord")
        weight = frame_window.astype(F32)
        coords, sums = project(frames, b_values, b_cols, weight)
        width, depth = coords.shape
        rows = width // m // CHUNKS
        stats = jnp.concatenate([sums[:2], jnp.full((1, width), jnp.sum(weight))])
        for j in range(n_f.bit_length() - 1):
            stats = stats + swap(stats, "frame", 1 << j)
        count = stats[2, 0]
        mean = stats[0] / count
        spread = jnp.maximum(stats[1] - stats[0] * mean, 1e-5 * stats[1])
        scale = lax.rsqrt(jnp.maximum(jnp.max(spread), 1e-30)) * 173.0
        mine = (weight[None, :] * (coords.astype(F32) - mean[:, None])).astype(BF16)

        own = mine.reshape(m, CHUNKS, rows, depth)
        panels = [[own[:, k] for k in range(CHUNKS)]]
        scales = [scale]
        for d in range(1, n_c):
            if d % 2:
                panels.append([swap(p, "coord", 1) for p in panels[d - 1]])
                scales.append(swap(scales[d - 1], "coord", 1))
            else:
                panels.append([swap(p, "coord", d) for p in panels[0]])
                scales.append(swap(scale, "coord", d))

        flip = (f // m) ^ c

        def gram(items, factors):
            left = jnp.concatenate(items)
            g = lax.dot_general(left, mine, (((1,), (1,)), ((), ())), preferred_element_type=F32)
            g = g.reshape(len(items), rows, width)
            return g * jnp.stack(factors)[:, None, None]

        def task(k, pair, order):
            def part(index):
                e = 0
                delta = 0
                for pos, what in enumerate(order):
                    bit = (index >> (len(order) - 1 - pos)) & 1
                    if what == "d":
                        delta = bit
                    else:
                        e |= bit << what
                a = e ^ (f % m)
                pick = ((flip & 1) ^ delta) == 1
                row = [lax.dynamic_index_in_dim(panels[2 * pair + i][k], a, 0, keepdims=False) for i in (0, 1)]
                factor = jnp.where(pick, scales[2 * pair + 1], scales[2 * pair]) * scale
                return jnp.where(pick, row[1], row[0]), factor

            n = 1 << len(order)
            parts = [part(i) for i in range(n)]
            send = gram(*zip(*parts[n // 2 :])).astype(F16)
            keep = gram(*zip(*parts[: n // 2]))
            for pos, what in enumerate(order):
                if pos:
                    half = keep.shape[0] // 2
                    send, keep = keep[half:].astype(F16), keep[:half]
                keep = keep + swap(send, "frame", m if what == "d" else 1 << what).astype(F32)
            return keep[0]

        first = ["d"] + list(range(low))
        second = list(range(low)) + ["d"]
        done = []
        for k in range(CHUNKS):
            order = first if k == 0 else second
            held = [task(k, pair, order) for pair in range(n_c // 2)]
            for j in range(1, high):
                pick = ((flip >> j) & 1) == 1
                lo = [held[i] for i in range(len(held)) if i % 2 == 0]
                hi = [held[i] for i in range(len(held)) if i % 2 == 1]
                held = [
                    jnp.where(pick, h, l)
                    + swap(jnp.where(pick, l, h).astype(F16), "frame", m << j).astype(F32)
                    for l, h in zip(lo, hi)
                ]
            done.append(held[0])
        row_scale = jnp.stack(scales)[flip]
        covariance = jnp.concatenate(done) * (1.0 / (row_scale * scale * (count - 1.0)))
        return count, mean, covariance

    return jax.shard_map(
        on_device,
        mesh=mesh,
        in_specs=(P("frame", None), P("coord", None), P("coord", None), P("frame")),
        out_specs=(P(), P("coord"), P("frame", "coord")),
        check_vma=False,
    )
```

```python
import jax
import jax.numpy as jnp
from jax import lax
from jax.experimental import pallas as pl
from jax.experimental.pallas import tpu as pltpu
from jax.sharding import PartitionSpec as P

BLOCK = 64
CHUNKS = 4
F32, F16, BF16 = jnp.float32, jnp.float16, jnp.bfloat16


def project_kernel(cols_ref, frames_ref, values_ref, window_ref, out_ref, sums_ref, dense_ref):
    row_blocks, nonzero = cols_ref.shape

    @pl.when(pl.program_id(0) == 0)
    def _():
        dense_ref[...] = jnp.zeros_like(dense_ref)
        sums_ref[...] = jnp.zeros_like(sums_ref)
        for r in range(0, row_blocks, 2):
            block = values_ref[r * BLOCK : (r + 2) * BLOCK, :].T
            for h in range(2):
                for k in range(nonzero):
                    start = pl.multiple_of(cols_ref[r + h, k] * BLOCK, BLOCK)
                    dense_ref[pl.ds(start, BLOCK), (r + h) * BLOCK : (r + h + 1) * BLOCK] = block[
                        k * BLOCK : (k + 1) * BLOCK, h * BLOCK : (h + 1) * BLOCK
                    ]

    product = jnp.dot(frames_ref[...], dense_ref[...], preferred_element_type=F32)
    coords = product.astype(BF16)
    out_ref[...] = coords.T
    window = window_ref[...].astype(F32)
    weight = jnp.broadcast_to(window, (8, window.shape[1])).astype(BF16)
    sums_ref[0:1, :] += jnp.dot(weight, coords, preferred_element_type=F32)[0:1]
    sums_ref[1:2, :] += jnp.dot(weight, coords * coords, preferred_element_type=F32)[0:1]
    count = jnp.sum(window, axis=1, keepdims=True)
    sums_ref[2:3, :] += jnp.broadcast_to(count, (1, coords.shape[1]))


def project(frames, values, cols, window):
    rows, cart = frames.shape
    width = values.shape[0]
    tile = min(256, rows)
    return pl.pallas_call(
        project_kernel,
        grid=(rows // tile,),
        in_specs=[
            pl.BlockSpec(memory_space=pltpu.SMEM),
            pl.BlockSpec((tile, cart), lambda i: (i, 0)),
            pl.BlockSpec(values.shape, lambda i: (0, 0)),
            pl.BlockSpec((1, tile), lambda i: (0, i)),
        ],
        out_specs=[
            pl.BlockSpec((width, tile), lambda i: (0, i)),
            pl.BlockSpec((8, width), lambda i: (0, 0)),
        ],
        out_shape=[
            jax.ShapeDtypeStruct((width, rows), BF16),
            jax.ShapeDtypeStruct((8, width), F32),
        ],
        scratch_shapes=[pltpu.VMEM((cart, width), BF16)],
        compiler_params=pltpu.CompilerParams(vmem_limit_bytes=48 * 2**20),
        cost_estimate=pl.CostEstimate(
            flops=2 * rows * cart * width, bytes_accessed=2 * rows * (cart + width), transcendentals=0
        ),
        name="project",
    )(cols, frames, values, window[None, :])


def gram_kernel(which_ref, group_ref, first_ref, second_ref, mine_ref, out_ref):
    part = pl.program_id(0)

    def write(left):
        out_ref[0] = lax.dot_general(
            left, mine_ref[...], (((1,), (1,)), ((), ())), preferred_element_type=F32
        )

    @pl.when(which_ref[part] == 0)
    def _():
        write(first_ref[0])

    @pl.when(which_ref[part] != 0)
    def _():
        write(second_ref[0])


def gram(which, group, first, second, mine):
    n = which.shape[0]
    _, rows, depth = first.shape
    width = mine.shape[0]
    return pl.pallas_call(
        gram_kernel,
        grid_spec=pltpu.PrefetchScalarGridSpec(
            num_scalar_prefetch=2,
            grid=(n,),
            in_specs=[
                pl.BlockSpec((1, rows, depth), lambda i, which, group: (group[i], 0, 0)),
                pl.BlockSpec((1, rows, depth), lambda i, which, group: (group[i], 0, 0)),
                pl.BlockSpec((width, depth), lambda i, which, group: (0, 0)),
            ],
            out_specs=pl.BlockSpec((1, rows, width), lambda i, which, group: (i, 0, 0)),
        ),
        out_shape=jax.ShapeDtypeStruct((n, rows, width), F32),
        compiler_params=pltpu.CompilerParams(vmem_limit_bytes=24 * 2**20),
        cost_estimate=pl.CostEstimate(flops=0, bytes_accessed=0, transcendentals=0),
        name="gram",
    )(which, group, first, second, mine)


def after(x, *gates):
    return lax.optimization_barrier((x,) + gates)[0] if gates else x


def solution(mesh):
    n_f, n_c = mesh.shape["frame"], mesh.shape["coord"]
    m = n_f // n_c
    low = m.bit_length() - 1
    high = n_c.bit_length() - 1
    n_pairs = n_c // 2

    def swap(x, axis, bit):
        return lax.ppermute(x, axis, [(i, i ^ bit) for i in range(mesh.shape[axis])])

    def on_device(frames, b_values, b_cols, frame_window):
        f, c = lax.axis_index("frame"), lax.axis_index("coord")
        coords, sums = project(frames, b_values, b_cols, frame_window)
        width, depth = coords.shape
        rows = width // m // CHUNKS
        for j in range(n_f.bit_length() - 1):
            sums = sums + swap(sums, "frame", 1 << j)
        count = sums[2, 0]
        mean = sums[0] / count
        spread = jnp.maximum(sums[1] - sums[0] * mean, 0.05 * sums[1] * (1.0 / 1024.0))
        largest = jnp.maximum(jnp.max(spread), 1e-30)
        scale = jnp.exp2(jnp.floor(0.5 * jnp.log2(16384.0 / largest)))
        weight = frame_window.astype(F32)
        centered = (weight[None, :] * (coords.astype(F32) - mean[:, None])).astype(BF16)
        mine = (centered.astype(F32) * scale).astype(BF16)

        flip = (f // m) ^ c
        own = mine.reshape(m, CHUNKS, rows, depth)
        panels = {}
        for k in range(CHUNKS):
            panels[0, k] = own[:, k]

        def near(k, *gates):
            panels[1, k] = swap(after(panels[0, k], *gates), "coord", 1)
            return panels[1, k]

        def far(k, *gates):
            for d in range(2, n_c, 2):
                panels[d, k] = swap(after(panels[0, k], *gates), "coord", d)
            return [panels[d, k] for d in range(2, n_c, 2)]

        def far_near(k, *gates):
            for d in range(2, n_c, 2):
                panels[d + 1, k] = swap(after(panels[d, k], *gates), "coord", 1)
            return [panels[d + 1, k] for d in range(2, n_c, 2)]

        class Task:
            def __init__(self, k, pair, order):
                self.order, self.at = order, 0
                n = 1 << len(order)
                which, group = [], []
                for index in range(n):
                    e, delta = 0, 0
                    for pos, what in enumerate(order):
                        bit = (index >> (len(order) - 1 - pos)) & 1
                        if what == "d":
                            delta = bit
                        else:
                            e |= bit << what
                    which.append((flip & 1) ^ delta)
                    group.append(e ^ (f % m))
                both = gram(
                    jnp.stack(which), jnp.stack(group), panels[2 * pair, k], panels[2 * pair + 1, k], mine
                )
                self.send = both[n // 2 :].astype(F16)
                self.keep = both[: n // 2]

            def step(self, *gates):
                what = self.order[self.at]
                if self.at:
                    half = self.keep.shape[0] // 2
                    self.send, self.keep = self.keep[half:].astype(F16), self.keep[:half]
                got = swap(after(self.send, *gates), "frame", m if what == "d" else 1 << what)
                self.keep = self.keep + got.astype(F32)
                self.at += 1
                return got

            def low_steps(self, *gates):
                for _ in range(low):
                    got = self.step(*gates)
                return got

        def tasks(k, far_pairs, order):
            return [Task(k, pair, order) for pair in (range(1, n_pairs) if far_pairs else range(1))]

        def low_steps(group, *gates):
            return [t.low_steps(*gates) for t in group]

        def d_step(group, *gates):
            return [t.step(*gates) for t in group]

        done = {}

        def top_steps(k, *gates):
            parts = [t.keep[0] for t in held[k, 0] + held[k, 1]]
            last = None
            for j in range(1, high):
                pick = ((flip >> j) & 1) == 1
                after_step = []
                for l, h in zip(parts[0::2], parts[1::2]):
                    last = swap(after(jnp.where(pick, l, h).astype(F16), *gates), "frame", m << j)
                    after_step.append(jnp.where(pick, h, l) + last.astype(F32))
                parts = after_step
            done[k] = parts[0]
            return last

        bits = list(range(low))
        low_first, d_first = bits + ["d"], ["d"] + bits
        held = {}
        x1 = far(1)
        near(1)
        near(2)
        near(0)
        near(3)
        x0 = far(0, panels[1, 1])

        def sends(k, far_pairs):
            return [t.send for t in held[k, far_pairs]]

        held[1, 0] = tasks(1, False, low_first)
        y0 = low_steps(held[1, 0])
        held[2, 0] = tasks(2, False, low_first)
        y1 = low_steps(held[2, 0])
        held[0, 0] = tasks(0, False, d_first)
        z00 = d_step(held[0, 0], *sends(1, 0))
        held[3, 0] = tasks(3, False, low_first)

        b0 = y0 + z00 + x1 + sends(2, 0)
        y2 = low_steps(held[0, 0], *b0)
        z10 = d_step(held[1, 0], *b0)
        c1 = far_near(1, *b0)
        x2 = far(2, *b0)
        held[1, 1] = tasks(1, True, low_first)

        b1 = y1 + z10 + x0 + c1 + sends(1, 1)
        c0 = far_near(0, *b1)
        z20 = d_step(held[2, 0], *b1)
        y3 = low_steps(held[1, 1], *b1)
        x3 = far(3, *b1)
        held[0, 1] = tasks(0, True, d_first)

        b2 = y2 + c0 + sends(0, 1) + sends(3, 0)
        z01 = d_step(held[0, 1], *b2)
        y4 = low_steps(held[3, 0], *b2)

        b3 = y3 + z20 + x2
        c2 = far_near(2, *b3)
        z11 = d_step(held[1, 1], *b3)
        held[2, 1] = tasks(2, True, low_first)

        b3b = z01 + z11
        y5 = low_steps(held[0, 1], *b3b)
        t1 = top_steps(1, *b3b)

        b4 = y4 + x3 + c2 + sends(2, 1)
        c3 = far_near(3, *b4)
        z30 = d_step(held[3, 0], *b4)
        y6 = low_steps(held[2, 1], *b4)
        held[3, 1] = tasks(3, True, low_first)

        b5 = y5 + z30 + [t1] + c3 + sends(3, 1)
        t0 = top_steps(0, *b5)
        y7 = low_steps(held[3, 1], *b5)

        b6 = y6
        z21 = d_step(held[2, 1], *b6)
        b6b = z21
        top_steps(2, *b6b)
        b7 = y7
        d_step(held[3, 1], *b7)
        top_steps(3)

        scales = [jnp.full((8, 128), scale)]
        for d in range(1, n_c):
            scales.append(swap(after(scales[d & ~1 if d % 2 else 0], *b4), "coord", 1 if d % 2 else d))
        row_scale = jnp.stack([s[0, 0] for s in scales])[flip]
        factor = 1.0 / (row_scale * scale * (count - 1.0))
        covariance = jnp.concatenate([done[k] * factor for k in range(CHUNKS)])
        return count, mean, covariance

    return jax.shard_map(
        on_device,
        mesh=mesh,
        in_specs=(P("frame", None), P("coord", None), P("coord", None), P("frame")),
        out_specs=(P(), P("coord"), P("frame", "coord")),
        check_vma=False,
    )
```

```python
import jax
import jax.numpy as jnp
from jax import lax
from jax.experimental import pallas as pl
from jax.experimental.pallas import tpu as pltpu
from jax.sharding import PartitionSpec as P

BLOCK = 64
CHUNKS = 2
F32, F16, BF16 = jnp.float32, jnp.float16, jnp.bfloat16


def project_kernel(cols_ref, frames_ref, values_ref, window_ref, out_ref, sums_ref, dense_ref):
    row_blocks, nonzero = cols_ref.shape

    @pl.when(pl.program_id(0) == 0)
    def _():
        dense_ref[...] = jnp.zeros_like(dense_ref)
        sums_ref[...] = jnp.zeros_like(sums_ref)
        for r in range(0, row_blocks, 2):
            block = values_ref[r * BLOCK : (r + 2) * BLOCK, :].T
            for h in range(2):
                for k in range(nonzero):
                    start = pl.multiple_of(cols_ref[r + h, k] * BLOCK, BLOCK)
                    dense_ref[pl.ds(start, BLOCK), (r + h) * BLOCK : (r + h + 1) * BLOCK] = block[
                        k * BLOCK : (k + 1) * BLOCK, h * BLOCK : (h + 1) * BLOCK
                    ]

    product = jnp.dot(frames_ref[...], dense_ref[...], preferred_element_type=F32)
    coords = product.astype(BF16)
    out_ref[...] = coords.T
    window = window_ref[...].astype(F32)
    weight = jnp.broadcast_to(window, (8, window.shape[1])).astype(BF16)
    sums_ref[0:1, :] += jnp.dot(weight, coords, preferred_element_type=F32)[0:1]
    sums_ref[1:2, :] += jnp.dot(weight, coords * coords, preferred_element_type=F32)[0:1]
    count = jnp.sum(window, axis=1, keepdims=True)
    sums_ref[2:3, :] += jnp.broadcast_to(count, (1, coords.shape[1]))


def project(frames, values, cols, window):
    rows, cart = frames.shape
    width = values.shape[0]
    tile = min(256, rows)
    return pl.pallas_call(
        project_kernel,
        grid=(rows // tile,),
        in_specs=[
            pl.BlockSpec(memory_space=pltpu.SMEM),
            pl.BlockSpec((tile, cart), lambda i: (i, 0)),
            pl.BlockSpec(values.shape, lambda i: (0, 0)),
            pl.BlockSpec((1, tile), lambda i: (0, i)),
        ],
        out_specs=[
            pl.BlockSpec((width, tile), lambda i: (0, i)),
            pl.BlockSpec((8, width), lambda i: (0, 0)),
        ],
        out_shape=[
            jax.ShapeDtypeStruct((width, rows), BF16),
            jax.ShapeDtypeStruct((8, width), F32),
        ],
        scratch_shapes=[pltpu.VMEM((cart, width), BF16)],
        compiler_params=pltpu.CompilerParams(vmem_limit_bytes=48 * 2**20),
        cost_estimate=pl.CostEstimate(
            flops=2 * rows * cart * width, bytes_accessed=2 * rows * (cart + width), transcendentals=0
        ),
        name="project",
    )(cols, frames, values, window[None, :])


def gram_kernel(which_ref, group_ref, half_ref, first_ref, second_ref, mine_ref, out_ref):
    part = pl.program_id(0)

    def write(left):
        out_ref[0] = lax.dot_general(
            left, mine_ref[...], (((1,), (1,)), ((), ())), preferred_element_type=F32
        )

    @pl.when(which_ref[part] == 0)
    def _():
        write(first_ref[0])

    @pl.when(which_ref[part] != 0)
    def _():
        write(second_ref[0])


def gram(which, group, half, first, second, mine):
    n = which.shape[0]
    _, rows, depth = first.shape
    width = mine.shape[0] // 2
    return pl.pallas_call(
        gram_kernel,
        grid_spec=pltpu.PrefetchScalarGridSpec(
            num_scalar_prefetch=3,
            grid=(n,),
            in_specs=[
                pl.BlockSpec((1, rows, depth), lambda i, which, group, half: (group[i], 0, 0)),
                pl.BlockSpec((1, rows, depth), lambda i, which, group, half: (group[i], 0, 0)),
                pl.BlockSpec((width, depth), lambda i, which, group, half: (half[i], 0)),
            ],
            out_specs=pl.BlockSpec((1, rows, width), lambda i, which, group, half: (i, 0, 0)),
        ),
        out_shape=jax.ShapeDtypeStruct((n, rows, width), F32),
        compiler_params=pltpu.CompilerParams(vmem_limit_bytes=24 * 2**20),
        cost_estimate=pl.CostEstimate(flops=0, bytes_accessed=0, transcendentals=0),
        name="gram",
    )(which, group, half, first, second, mine)


def assemble_kernel(flags_ref, direct_ref, mirror_ref, diagonal_ref, factor_ref, out_ref):
    groups, _, group_width = mirror_ref.shape
    half_width = direct_ref.shape[1]
    factor = factor_ref[0:1, 0:1]
    second = flags_ref[0] != 0

    def write(begin, value):
        out_ref[:, begin : begin + value.shape[1]] = value * factor

    def write_other(begin):
        @pl.when(flags_ref[1] != 0)
        def _():
            write(begin, diagonal_ref[...])

        @pl.when(flags_ref[1] == 0)
        def _():
            for pos in range(groups):
                write(begin + pos * group_width, mirror_ref[pos ^ flags_ref[2]].T)

    @pl.when(second)
    def _():
        write(half_width, direct_ref[...])
        write_other(0)

    @pl.when(jnp.logical_not(second))
    def _():
        write(0, direct_ref[...])
        write_other(half_width)


def assemble(flags, direct, mirror, diagonal, factor):
    rows, half_width = direct.shape
    return pl.pallas_call(
        assemble_kernel,
        in_specs=[pl.BlockSpec(memory_space=pltpu.SMEM)]
        + [pl.BlockSpec(memory_space=pltpu.VMEM)] * 4,
        out_specs=pl.BlockSpec(memory_space=pltpu.VMEM),
        out_shape=jax.ShapeDtypeStruct((rows, 2 * half_width), F32),
        compiler_params=pltpu.CompilerParams(vmem_limit_bytes=32 * 2**20),
        name="assemble",
    )(flags, direct, mirror, diagonal, factor)


def moments_kernel(sums_ref, out_ref):
    total, squares, count = sums_ref[0:1, :], sums_ref[1:2, :], sums_ref[2:3, :]
    mean = total / count
    spread = jnp.maximum(squares - total * mean, squares * (0.05 / 1024.0))
    largest = jnp.maximum(jnp.max(spread, axis=1, keepdims=True), 1e-30)
    scale = jnp.exp2(jnp.floor(0.5 * jnp.log2(16384.0 / largest)))
    out_ref[...] = jnp.zeros_like(out_ref)
    out_ref[0:1, :] = mean
    out_ref[1:2, :] = jnp.broadcast_to(scale, mean.shape)
    out_ref[2:3, :] = count


def moments(sums):
    return pl.pallas_call(
        moments_kernel,
        in_specs=[pl.BlockSpec(memory_space=pltpu.VMEM)],
        out_specs=pl.BlockSpec(memory_space=pltpu.VMEM),
        out_shape=jax.ShapeDtypeStruct(sums.shape, F32),
        name="moments",
    )(sums)


def after(x, *gates):
    return lax.optimization_barrier((x,) + gates)[0] if gates else x


def solution(mesh):
    n_f, n_c = mesh.shape["frame"], mesh.shape["coord"]
    m = n_f // n_c
    low = m.bit_length() - 1
    high = n_c.bit_length() - 1
    n_pairs = n_c // 2

    def swap(x, axis, bit):
        return lax.ppermute(x, axis, [(i, i ^ bit) for i in range(mesh.shape[axis])])

    def on_device(frames, b_values, b_cols, frame_window):
        f, c = lax.axis_index("frame"), lax.axis_index("coord")
        coords, sums = project(frames, b_values, b_cols, frame_window)
        width, depth = coords.shape
        rows = width // m // CHUNKS
        raw = coords.reshape(m, CHUNKS, rows, depth)
        raw_far = {(d, 0): swap(raw[:, 0], "coord", d) for d in range(2, n_c, 2)}
        for j in range(n_f.bit_length() - 1):
            sums = sums + swap(sums, "frame", 1 << j)
        pack = moments(sums)
        mean, scale, count = pack[0], pack[1, 0], pack[2, 0]
        weight = frame_window.astype(F32)

        def center(x, mean, scale):
            centered = (weight * (x.astype(F32) - mean[..., None])).astype(BF16)
            return (centered.astype(F32) * scale).astype(BF16)

        mine = center(coords, mean, scale)
        packs = {0: pack, 1: swap(pack, "coord", 1)}
        for d in range(2, n_c, 2):
            packs[d] = swap(pack, "coord", d)
            for k in range(1, CHUNKS):
                raw_far[d, k] = swap(after(raw[:, k], pack), "coord", d)
            packs[d + 1] = swap(packs[d], "coord", 1)

        flip = (f // m) ^ c
        a = f % m
        top = low - 1

        def direct_half(group, d):
            return (group >> top) ^ ((c ^ d) > c).astype(jnp.int32)

        own = mine.reshape(m, CHUNKS, rows, depth)
        panels = {}
        for k in range(CHUNKS):
            panels[0, k] = own[:, k]

        def near(k, *gates):
            panels[1, k] = swap(after(panels[0, k], *gates), "coord", 1)
            return panels[1, k]

        def far(k, *gates):
            for d in range(2, n_c, 2):
                mean_k = packs[d][0].reshape(m, CHUNKS, rows)[:, k]
                panels[d, k] = center(after(raw_far[d, k], *gates), mean_k, packs[d][1, 0])
            return [panels[d, k] for d in range(2, n_c, 2)]

        def far_near(k, *gates):
            for d in range(2, n_c, 2):
                panels[d + 1, k] = swap(after(panels[d, k], *gates), "coord", 1)
            return [panels[d + 1, k] for d in range(2, n_c, 2)]

        class Task:
            def __init__(self, k, pair, order):
                self.order, self.at = order, 0
                n = 1 << len(order)
                which, group, half = [], [], []
                for index in range(n):
                    e, delta = 0, 0
                    for pos, what in enumerate(order):
                        bit = (index >> (len(order) - 1 - pos)) & 1
                        if what == "d":
                            delta = bit
                        else:
                            e |= bit << what
                    which.append((flip & 1) ^ delta)
                    group.append(e ^ a)
                    half.append(direct_half(group[-1], 2 * pair + which[-1]))
                both = gram(
                    jnp.stack(which),
                    jnp.stack(group),
                    jnp.stack(half),
                    panels[2 * pair, k],
                    panels[2 * pair + 1, k],
                    mine,
                )
                self.send = both[n // 2 :].astype(F16)
                self.keep = both[: n // 2]

            def step(self, *gates):
                what = self.order[self.at]
                if self.at:
                    half = self.keep.shape[0] // 2
                    self.send, self.keep = self.keep[half:].astype(F16), self.keep[:half]
                got = swap(after(self.send, *gates), "frame", m if what == "d" else 1 << what)
                self.keep = self.keep + got.astype(F32)
                self.at += 1
                return got

            def low_steps(self, *gates):
                for _ in range(low):
                    got = self.step(*gates)
                return got

        def tasks(k, far_pairs, order):
            return [Task(k, pair, order) for pair in (range(1, n_pairs) if far_pairs else range(1))]

        def low_steps(group, *gates):
            return [t.low_steps(*gates) for t in group]

        def d_step(group, *gates):
            return [t.step(*gates) for t in group]

        done = {}

        def top_steps(k, *gates):
            parts = [t.keep[0] for t in held[k, 0] + held[k, 1]]
            last = None
            for j in range(1, high):
                pick = ((flip >> j) & 1) == 1
                after_step = []
                for l, h in zip(parts[0::2], parts[1::2]):
                    last = swap(after(jnp.where(pick, l, h).astype(F16), *gates), "frame", m << j)
                    after_step.append(jnp.where(pick, h, l) + last.astype(F32))
                parts = after_step
            done[k] = parts[0]
            return last

        def directed(x, pairs, *gates):
            return lax.ppermute(after(x, *gates), ("frame", "coord"), pairs)

        class Diagonal:
            def __init__(self):
                group = [e ^ a for e in range(m)]
                whole = mine.reshape(m, CHUNKS * rows, depth)
                half = [(g >> top) ^ 1 for g in group]
                zero = jnp.zeros((m,), jnp.int32)
                both = gram(zero, jnp.stack(group), jnp.stack(half), whole, whole, mine)
                self.keep, self.send = both[: m // 2], both[m // 2 :].astype(F16)

            def low_steps(self, *gates):
                for j in reversed(range(low)):
                    if j < top:
                        half = self.keep.shape[0] // 2
                        self.keep, self.send = self.keep[:half], self.keep[half:].astype(F16)
                    got = swap(after(self.send, *gates), "frame", 1 << j)
                    self.keep = self.keep + got.astype(F32)
                return [got]

            def panel_step(self, j, *gates):
                pairs = []
                for g in range(n_f):
                    for d in range(n_c):
                        if (((g // m) ^ d) & ((2 << j) - 1)) == 1 << j:
                            pairs.append((g * n_c + d, (g ^ (m << j)) * n_c + d))
                got = directed(self.keep.astype(F16), pairs, *gates)
                self.keep = self.keep + got.astype(F32)
                return [got]

        mirrored = {}

        def mirror(k, *gates):
            group_width = CHUNKS * rows
            for i in range(m // 2):
                pairs = []
                for r in range(n_c):
                    for g in range(m):
                        for d in range(n_c):
                            if r != d:
                                there = (((g >> top) ^ (r > d)) << top) | ((g & (m // 2 - 1)) ^ i)
                                pairs.append(((r * m + g) * n_c + d, (d * m + there) * n_c + r))
                begin = ((a & (m // 2 - 1)) ^ i) * group_width
                block = done[k] if m == 2 else lax.dynamic_slice_in_dim(done[k], begin, group_width, 1)
                mirrored[i, k] = directed(block.astype(F16), pairs, *gates)
            return [mirrored[i, k] for i in range(m // 2)]

        low_first = list(reversed(range(low))) + ["d"]
        d_first = ["d"] + list(reversed(range(low)))
        held = {}

        def sends(k, far_pairs):
            return [t.send for t in held[k, far_pairs]]

        row_scale = pack[:, :128]
        for d in range(1, n_c):
            row_scale = jnp.where(flip == d, packs[d][:, :128], row_scale)
        row_scale = row_scale[1:2]
        factor = 1.0 / (row_scale * scale * (count - 1.0))

        near(0)
        near(1)
        diagonal = Diagonal()
        ye = diagonal.low_steps()
        held[0, 0] = tasks(0, False, d_first)
        z00 = d_step(held[0, 0], diagonal.send)
        held[1, 0] = tasks(1, False, low_first)
        y10 = low_steps(held[1, 0], *sends(0, 0))
        far(0)
        far_near(0)
        held[0, 1] = tasks(0, True, d_first)

        ze = diagonal.panel_step(0, *(ye + sends(0, 0) + sends(1, 0)))
        b0 = ye + z00 + sends(1, 0) + sends(0, 1)
        y00 = low_steps(held[0, 0], *b0)
        z01 = d_step(held[0, 1], *b0)
        for j in range(1, high):
            te = diagonal.panel_step(j, *(ze + b0))
        far(1, *b0)
        far_near(1)
        held[1, 1] = tasks(1, True, low_first)

        b1 = z01 + y10 + y00 + te + sends(1, 1) + [factor]
        y01 = low_steps(held[0, 1], *b1)
        y11 = low_steps(held[1, 1], *y01)
        z10 = d_step(held[1, 0], *y01)

        t0 = top_steps(0, *y01)

        b3 = y11 + [t0] + z10
        z11 = d_step(held[1, 1], *b3)
        m0 = mirror(0)
        top_steps(1, *(z11 + m0))
        mirror(1)

        direct = jnp.concatenate([done[k] for k in range(CHUNKS)])
        blocks = jnp.stack(
            [jnp.concatenate([mirrored[i, k] for k in range(CHUNKS)]).astype(F32) for i in range(m // 2)]
        )
        flags = jnp.stack(
            [direct_half(a, flip), (flip == 0).astype(jnp.int32), a & (m // 2 - 1)]
        )
        covariance = assemble(
            flags, direct, blocks, diagonal.keep[0], factor
        )
        return count, mean, covariance

    return jax.shard_map(
        on_device,
        mesh=mesh,
        in_specs=(P("frame", None), P("coord", None), P("coord", None), P("frame")),
        out_specs=(P(), P("coord"), P("frame", "coord")),
        check_vma=False,
    )
```

```python
import jax
import jax.numpy as jnp
from jax import lax
from jax.experimental import pallas as pl
from jax.experimental.pallas import tpu as pltpu
from jax.sharding import PartitionSpec as P

BLOCK = 64
CHUNKS = 2
F32, F16, BF16 = jnp.float32, jnp.float16, jnp.bfloat16


def project_kernel(cols_ref, frames_ref, values_ref, window_ref, out_ref, sums_ref, dense_ref):
    row_blocks, nonzero = cols_ref.shape

    @pl.when(pl.program_id(0) == 0)
    def _():
        dense_ref[...] = jnp.zeros_like(dense_ref)
        sums_ref[...] = jnp.zeros_like(sums_ref)
        for r in range(0, row_blocks, 2):
            block = values_ref[r * BLOCK : (r + 2) * BLOCK, :].T
            for h in range(2):
                for k in range(nonzero):
                    start = pl.multiple_of(cols_ref[r + h, k] * BLOCK, BLOCK)
                    dense_ref[pl.ds(start, BLOCK), (r + h) * BLOCK : (r + h + 1) * BLOCK] = block[
                        k * BLOCK : (k + 1) * BLOCK, h * BLOCK : (h + 1) * BLOCK
                    ]

    product = jnp.dot(frames_ref[...], dense_ref[...], preferred_element_type=F32)
    coords = product.astype(BF16)
    out_ref[...] = coords.T
    window = window_ref[...].astype(F32)
    weight = jnp.broadcast_to(window, (8, window.shape[1])).astype(BF16)
    sums_ref[0:1, :] += jnp.dot(weight, coords, preferred_element_type=F32)[0:1]
    sums_ref[1:2, :] += jnp.dot(weight, coords * coords, preferred_element_type=F32)[0:1]
    count = jnp.sum(window, axis=1, keepdims=True)
    sums_ref[2:3, :] += jnp.broadcast_to(count, (1, coords.shape[1]))


def project(frames, values, cols, window):
    rows, cart = frames.shape
    width = values.shape[0]
    tile = min(256, rows)
    return pl.pallas_call(
        project_kernel,
        grid=(rows // tile,),
        in_specs=[
            pl.BlockSpec(memory_space=pltpu.SMEM),
            pl.BlockSpec((tile, cart), lambda i: (i, 0)),
            pl.BlockSpec(values.shape, lambda i: (0, 0)),
            pl.BlockSpec((1, tile), lambda i: (0, i)),
        ],
        out_specs=[
            pl.BlockSpec((width, tile), lambda i: (0, i)),
            pl.BlockSpec((8, width), lambda i: (0, 0)),
        ],
        out_shape=[
            jax.ShapeDtypeStruct((width, rows), BF16),
            jax.ShapeDtypeStruct((8, width), F32),
        ],
        scratch_shapes=[pltpu.VMEM((cart, width), BF16)],
        compiler_params=pltpu.CompilerParams(vmem_limit_bytes=48 * 2**20),
        cost_estimate=pl.CostEstimate(
            flops=2 * rows * cart * width, bytes_accessed=2 * rows * (cart + width), transcendentals=0
        ),
        name="project",
    )(cols, frames, values, window[None, :])


def gram_kernel(which_ref, group_ref, half_ref, first_ref, second_ref, mine_ref, out_ref):
    part = pl.program_id(0)

    def write(left):
        out_ref[0] = lax.dot_general(
            left, mine_ref[...], (((1,), (1,)), ((), ())), preferred_element_type=F32
        )

    @pl.when(which_ref[part] == 0)
    def _():
        write(first_ref[0])

    @pl.when(which_ref[part] != 0)
    def _():
        write(second_ref[0])


def gram(which, group, half, first, second, mine):
    n = which.shape[0]
    _, rows, depth = first.shape
    width = mine.shape[0] // 2
    return pl.pallas_call(
        gram_kernel,
        grid_spec=pltpu.PrefetchScalarGridSpec(
            num_scalar_prefetch=3,
            grid=(n,),
            in_specs=[
                pl.BlockSpec((1, rows, depth), lambda i, which, group, half: (group[i], 0, 0)),
                pl.BlockSpec((1, rows, depth), lambda i, which, group, half: (group[i], 0, 0)),
                pl.BlockSpec((width, depth), lambda i, which, group, half: (half[i], 0)),
            ],
            out_specs=pl.BlockSpec((1, rows, width), lambda i, which, group, half: (i, 0, 0)),
        ),
        out_shape=jax.ShapeDtypeStruct((n, rows, width), F32),
        compiler_params=pltpu.CompilerParams(vmem_limit_bytes=24 * 2**20),
        cost_estimate=pl.CostEstimate(flops=0, bytes_accessed=0, transcendentals=0),
        name="gram",
    )(which, group, half, first, second, mine)


def assemble_kernel(flags_ref, direct_ref, mirror_ref, diagonal_ref, factor_ref, out_ref):
    groups, _, group_width = mirror_ref.shape
    half_width = direct_ref.shape[1]
    factor = factor_ref[0:1, 0:1]
    second = flags_ref[0] != 0

    def write(begin, value):
        out_ref[:, begin : begin + value.shape[1]] = value * factor

    def write_other(begin):
        @pl.when(flags_ref[1] != 0)
        def _():
            write(begin, diagonal_ref[...])

        @pl.when(flags_ref[1] == 0)
        def _():
            for pos in range(groups):
                write(begin + pos * group_width, mirror_ref[pos ^ flags_ref[2]].T)

    @pl.when(second)
    def _():
        write(half_width, direct_ref[...])
        write_other(0)

    @pl.when(jnp.logical_not(second))
    def _():
        write(0, direct_ref[...])
        write_other(half_width)


def assemble(flags, direct, mirror, diagonal, factor):
    rows, half_width = direct.shape
    return pl.pallas_call(
        assemble_kernel,
        in_specs=[pl.BlockSpec(memory_space=pltpu.SMEM)]
        + [pl.BlockSpec(memory_space=pltpu.VMEM)] * 4,
        out_specs=pl.BlockSpec(memory_space=pltpu.VMEM),
        out_shape=jax.ShapeDtypeStruct((rows, 2 * half_width), F32),
        compiler_params=pltpu.CompilerParams(vmem_limit_bytes=32 * 2**20),
        name="assemble",
    )(flags, direct, mirror, diagonal, factor)


def moments_kernel(sums_ref, out_ref):
    total, squares, count = sums_ref[0:1, :], sums_ref[1:2, :], sums_ref[2:3, :]
    mean = total / count
    spread = jnp.maximum(squares - total * mean, 0.0) + squares * (1.0 / 128.0)
    largest = jnp.maximum(jnp.max(spread, axis=1, keepdims=True), 1e-30)
    scale = jnp.exp2(jnp.floor(0.5 * jnp.log2(16384.0 / largest)))
    out_ref[...] = jnp.zeros_like(out_ref)
    out_ref[0:1, :] = mean
    out_ref[1:2, :] = jnp.broadcast_to(scale, mean.shape)
    out_ref[2:3, :] = count


def moments(sums):
    return pl.pallas_call(
        moments_kernel,
        in_specs=[pl.BlockSpec(memory_space=pltpu.VMEM)],
        out_specs=pl.BlockSpec(memory_space=pltpu.VMEM),
        out_shape=jax.ShapeDtypeStruct(sums.shape, F32),
        name="moments",
    )(sums)


def after(x, *gates):
    return lax.optimization_barrier((x,) + gates)[0] if gates else x


def solution(mesh):
    n_f, n_c = mesh.shape["frame"], mesh.shape["coord"]
    m = n_f // n_c
    low = m.bit_length() - 1
    high = n_c.bit_length() - 1
    n_pairs = n_c // 2

    def swap(x, axis, bit):
        return lax.ppermute(x, axis, [(i, i ^ bit) for i in range(mesh.shape[axis])])

    def on_device(frames, b_values, b_cols, frame_window):
        f, c = lax.axis_index("frame"), lax.axis_index("coord")
        coords, sums = project(frames, b_values, b_cols, frame_window)
        width, depth = coords.shape
        rows = width // m // CHUNKS
        raw = coords.reshape(m, CHUNKS, rows, depth)
        raw_far = {(d, 0): swap(raw[:, 0], "coord", d) for d in range(2, n_c, 2)}
        for j in range(n_f.bit_length() - 1):
            sums = sums + swap(sums, "frame", 1 << j)
        pack = moments(sums)
        mean, scale, count = pack[0], pack[1, 0], pack[2, 0]
        weight = frame_window.astype(F32)

        def center(x, mean, scale):
            centered = (weight * (x.astype(F32) - mean[..., None])).astype(BF16)
            return (centered.astype(F32) * scale).astype(BF16)

        mine = center(coords, mean, scale)
        packs = {0: pack, 1: swap(pack, "coord", 1)}
        for d in range(2, n_c, 2):
            packs[d] = swap(pack, "coord", d)
            for k in range(1, CHUNKS):
                raw_far[d, k] = swap(after(raw[:, k], pack), "coord", d)
            packs[d + 1] = swap(packs[d], "coord", 1)

        flip = (f // m) ^ c
        a = f % m
        top = low - 1

        def direct_half(group, d):
            return (group >> top) ^ ((c ^ d) > c).astype(jnp.int32)

        own = mine.reshape(m, CHUNKS, rows, depth)
        panels = {}
        for k in range(CHUNKS):
            panels[0, k] = own[:, k]

        def near(k, *gates):
            panels[1, k] = swap(after(panels[0, k], *gates), "coord", 1)
            return panels[1, k]

        def far(k, *gates):
            for d in range(2, n_c, 2):
                mean_k = packs[d][0].reshape(m, CHUNKS, rows)[:, k]
                panels[d, k] = center(after(raw_far[d, k], *gates), mean_k, packs[d][1, 0])
            return [panels[d, k] for d in range(2, n_c, 2)]

        def far_near(k, *gates):
            for d in range(2, n_c, 2):
                panels[d + 1, k] = swap(after(panels[d, k], *gates), "coord", 1)
            return [panels[d + 1, k] for d in range(2, n_c, 2)]

        class Task:
            def __init__(self, k, pair, order):
                self.order, self.at = order, 0
                n = 1 << len(order)
                which, group, half = [], [], []
                for index in range(n):
                    e, delta = 0, 0
                    for pos, what in enumerate(order):
                        bit = (index >> (len(order) - 1 - pos)) & 1
                        if what == "d":
                            delta = bit
                        else:
                            e |= bit << what
                    which.append((flip & 1) ^ delta)
                    group.append(e ^ a)
                    half.append(direct_half(group[-1], 2 * pair + which[-1]))
                both = gram(
                    jnp.stack(which),
                    jnp.stack(group),
                    jnp.stack(half),
                    panels[2 * pair, k],
                    panels[2 * pair + 1, k],
                    mine,
                )
                self.send = both[n // 2 :].astype(F16)
                self.keep = both[: n // 2]

            def step(self, *gates):
                what = self.order[self.at]
                if self.at:
                    half = self.keep.shape[0] // 2
                    self.send, self.keep = self.keep[half:].astype(F16), self.keep[:half]
                got = swap(after(self.send, *gates), "frame", m if what == "d" else 1 << what)
                self.keep = self.keep + got.astype(F32)
                self.at += 1
                return got

            def low_steps(self, *gates):
                for _ in range(low):
                    got = self.step(*gates)
                return got

        def tasks(k, far_pairs, order):
            return [Task(k, pair, order) for pair in (range(1, n_pairs) if far_pairs else range(1))]

        def low_steps(group, *gates):
            return [t.low_steps(*gates) for t in group]

        def d_step(group, *gates):
            return [t.step(*gates) for t in group]

        done = {}

        def top_steps(k, *gates):
            parts = [t.keep[0] for t in held[k, 0] + held[k, 1]]
            last = None
            for j in range(1, high):
                pick = ((flip >> j) & 1) == 1
                after_step = []
                for l, h in zip(parts[0::2], parts[1::2]):
                    last = swap(after(jnp.where(pick, l, h).astype(F16), *gates), "frame", m << j)
                    after_step.append(jnp.where(pick, h, l) + last.astype(F32))
                parts = after_step
            done[k] = parts[0]
            return last

        def directed(x, pairs, *gates):
            return lax.ppermute(after(x, *gates), ("frame", "coord"), pairs)

        class Diagonal:
            def __init__(self):
                group = [e ^ a for e in range(m)]
                whole = mine.reshape(m, CHUNKS * rows, depth)
                half = [(g >> top) ^ 1 for g in group]
                zero = jnp.zeros((m,), jnp.int32)
                both = gram(zero, jnp.stack(group), jnp.stack(half), whole, whole, mine)
                self.keep, self.send = both[: m // 2], both[m // 2 :].astype(F16)

            def low_steps(self, *gates):
                for j in reversed(range(low)):
                    if j < top:
                        half = self.keep.shape[0] // 2
                        self.keep, self.send = self.keep[:half], self.keep[half:].astype(F16)
                    got = swap(after(self.send, *gates), "frame", 1 << j)
                    self.keep = self.keep + got.astype(F32)
                return [got]

            def panel_step(self, j, *gates):
                pairs = []
                for g in range(n_f):
                    for d in range(n_c):
                        if (((g // m) ^ d) & ((2 << j) - 1)) == 1 << j:
                            pairs.append((g * n_c + d, (g ^ (m << j)) * n_c + d))
                got = directed(self.keep.astype(F16), pairs, *gates)
                self.keep = self.keep + got.astype(F32)
                return [got]

        mirrored = {}

        def mirror(k, *gates):
            group_width = CHUNKS * rows
            for i in range(m // 2):
                pairs = []
                for r in range(n_c):
                    for g in range(m):
                        for d in range(n_c):
                            if r != d:
                                there = (((g >> top) ^ (r > d)) << top) | ((g & (m // 2 - 1)) ^ i)
                                pairs.append(((r * m + g) * n_c + d, (d * m + there) * n_c + r))
                begin = ((a & (m // 2 - 1)) ^ i) * group_width
                block = done[k] if m == 2 else lax.dynamic_slice_in_dim(done[k], begin, group_width, 1)
                mirrored[i, k] = directed(block.astype(F16), pairs, *gates)
            return [mirrored[i, k] for i in range(m // 2)]

        low_first = list(reversed(range(low))) + ["d"]
        d_first = ["d"] + list(reversed(range(low)))
        held = {}

        def sends(k, far_pairs):
            return [t.send for t in held[k, far_pairs]]

        row_scale = pack[:, :128]
        for d in range(1, n_c):
            row_scale = jnp.where(flip == d, packs[d][:, :128], row_scale)
        row_scale = row_scale[1:2]
        factor = 1.0 / (row_scale * scale * (count - 1.0))

        near(0)
        near(1)
        diagonal = Diagonal()
        ye = diagonal.low_steps()
        held[0, 0] = tasks(0, False, d_first)
        z00 = d_step(held[0, 0], diagonal.send)
        held[1, 0] = tasks(1, False, low_first)
        y10 = low_steps(held[1, 0], *sends(0, 0))
        far(0)
        far_near(0)
        held[0, 1] = tasks(0, True, d_first)

        ze = diagonal.panel_step(0, *(ye + sends(0, 0) + sends(1, 0)))
        b0 = ye + z00 + sends(1, 0) + sends(0, 1)
        y00 = low_steps(held[0, 0], *b0)
        z01 = d_step(held[0, 1], *b0)
        for j in range(1, high):
            te = diagonal.panel_step(j, *(ze + b0))
        far(1, *b0)
        far_near(1)
        held[1, 1] = tasks(1, True, low_first)

        b1 = z01 + y10 + y00 + te + sends(1, 1) + [factor]
        y01 = low_steps(held[0, 1], *b1)
        y11 = low_steps(held[1, 1], *y01)
        z10 = d_step(held[1, 0], *y01)

        t0 = top_steps(0, *y01)

        b3 = y11 + [t0] + z10
        z11 = d_step(held[1, 1], *b3)
        m0 = mirror(0)
        top_steps(1, *(z11 + m0))
        mirror(1)

        direct = jnp.concatenate([done[k] for k in range(CHUNKS)])
        blocks = jnp.stack(
            [jnp.concatenate([mirrored[i, k] for k in range(CHUNKS)]).astype(F32) for i in range(m // 2)]
        )
        flags = jnp.stack(
            [direct_half(a, flip), (flip == 0).astype(jnp.int32), a & (m // 2 - 1)]
        )
        covariance = assemble(
            flags, direct, blocks, diagonal.keep[0], factor
        )
        return count, mean, covariance

    return jax.shard_map(
        on_device,
        mesh=mesh,
        in_specs=(P("frame", None), P("coord", None), P("coord", None), P("frame")),
        out_specs=(P(), P("coord"), P("frame", "coord")),
        check_vma=False,
    )
```

```python
import functools

import jax
import jax.numpy as jnp
from jax import lax
from jax.experimental import pallas as pl
from jax.experimental.pallas import tpu as pltpu
from jax.sharding import PartitionSpec as P

BLOCK = 64
CHUNKS = 2
F32, F16, BF16 = jnp.float32, jnp.float16, jnp.bfloat16


def project_kernel(cols_ref, frames_ref, values_ref, window_ref, out_ref, sums_ref, dense_ref):
    row_blocks, nonzero = cols_ref.shape

    @pl.when(pl.program_id(0) == 0)
    def _():
        dense_ref[...] = jnp.zeros_like(dense_ref)
        sums_ref[...] = jnp.zeros_like(sums_ref)
        for r in range(0, row_blocks, 2):
            block = values_ref[r * BLOCK : (r + 2) * BLOCK, :].T
            for h in range(2):
                for k in range(nonzero):
                    start = pl.multiple_of(cols_ref[r + h, k] * BLOCK, BLOCK)
                    dense_ref[pl.ds(start, BLOCK), (r + h) * BLOCK : (r + h + 1) * BLOCK] = block[
                        k * BLOCK : (k + 1) * BLOCK, h * BLOCK : (h + 1) * BLOCK
                    ]

    product = jnp.dot(frames_ref[...], dense_ref[...], preferred_element_type=F32)
    coords = product.astype(BF16)
    out_ref[...] = coords.T
    window = window_ref[...].astype(F32)
    weight = jnp.broadcast_to(window, (8, window.shape[1])).astype(BF16)
    sums_ref[0:1, :] += jnp.dot(weight, coords, preferred_element_type=F32)[0:1]
    sums_ref[1:2, :] += jnp.dot(weight, coords * coords, preferred_element_type=F32)[0:1]
    count = jnp.sum(window, axis=1, keepdims=True)
    sums_ref[2:3, :] += jnp.broadcast_to(count, (1, coords.shape[1]))


def project(frames, values, cols, window):
    rows, cart = frames.shape
    width = values.shape[0]
    tile = min(256, rows)
    return pl.pallas_call(
        project_kernel,
        grid=(rows // tile,),
        in_specs=[
            pl.BlockSpec(memory_space=pltpu.SMEM),
            pl.BlockSpec((tile, cart), lambda i: (i, 0)),
            pl.BlockSpec(values.shape, lambda i: (0, 0)),
            pl.BlockSpec((1, tile), lambda i: (0, i)),
        ],
        out_specs=[
            pl.BlockSpec((width, tile), lambda i: (0, i)),
            pl.BlockSpec((8, width), lambda i: (0, 0)),
        ],
        out_shape=[
            jax.ShapeDtypeStruct((width, rows), BF16),
            jax.ShapeDtypeStruct((8, width), F32),
        ],
        scratch_shapes=[pltpu.VMEM((cart, width), BF16)],
        compiler_params=pltpu.CompilerParams(vmem_limit_bytes=48 * 2**20),
        cost_estimate=pl.CostEstimate(
            flops=2 * rows * cart * width, bytes_accessed=2 * rows * (cart + width), transcendentals=0
        ),
        name="project",
    )(cols, frames, values, window[None, :])


def gram_kernel(which_ref, group_ref, half_ref, first_ref, second_ref, mine_ref, out_ref):
    part = pl.program_id(0)

    def write(left):
        out_ref[0] = lax.dot_general(
            left, mine_ref[...], (((1,), (1,)), ((), ())), preferred_element_type=F32
        )

    @pl.when(which_ref[part] == 0)
    def _():
        write(first_ref[0])

    @pl.when(which_ref[part] != 0)
    def _():
        write(second_ref[0])


def gram(which, group, half, first, second, mine):
    n = which.shape[0]
    _, rows, depth = first.shape
    width = mine.shape[0] // 2
    return pl.pallas_call(
        gram_kernel,
        grid_spec=pltpu.PrefetchScalarGridSpec(
            num_scalar_prefetch=3,
            grid=(n,),
            in_specs=[
                pl.BlockSpec((1, rows, depth), lambda i, which, group, half: (group[i], 0, 0)),
                pl.BlockSpec((1, rows, depth), lambda i, which, group, half: (group[i], 0, 0)),
                pl.BlockSpec((width, depth), lambda i, which, group, half: (half[i], 0)),
            ],
            out_specs=pl.BlockSpec((1, rows, width), lambda i, which, group, half: (i, 0, 0)),
        ),
        out_shape=jax.ShapeDtypeStruct((n, rows, width), F32),
        compiler_params=pltpu.CompilerParams(vmem_limit_bytes=24 * 2**20),
        cost_estimate=pl.CostEstimate(flops=0, bytes_accessed=0, transcendentals=0),
        name="gram",
    )(which, group, half, first, second, mine)


def assemble_kernel(flags_ref, direct_ref, mirror_ref, diagonal_ref, factor_ref, out_ref):
    groups, _, group_width = mirror_ref.shape
    half_width = direct_ref.shape[1]
    factor = factor_ref[0:1, 0:1]
    second = flags_ref[0] != 0

    def write(begin, value):
        out_ref[:, begin : begin + value.shape[1]] = value * factor

    def write_other(begin):
        @pl.when(flags_ref[1] != 0)
        def _():
            write(begin, diagonal_ref[...])

        @pl.when(flags_ref[1] == 0)
        def _():
            for pos in range(groups):
                write(begin + pos * group_width, mirror_ref[pos ^ flags_ref[2]].T)

    @pl.when(second)
    def _():
        write(half_width, direct_ref[...])
        write_other(0)

    @pl.when(jnp.logical_not(second))
    def _():
        write(0, direct_ref[...])
        write_other(half_width)


def assemble(flags, direct, mirror, diagonal, factor):
    rows, half_width = direct.shape
    return pl.pallas_call(
        assemble_kernel,
        in_specs=[pl.BlockSpec(memory_space=pltpu.SMEM)]
        + [pl.BlockSpec(memory_space=pltpu.VMEM)] * 4,
        out_specs=pl.BlockSpec(memory_space=pltpu.VMEM),
        out_shape=jax.ShapeDtypeStruct((rows, 2 * half_width), F32),
        compiler_params=pltpu.CompilerParams(vmem_limit_bytes=32 * 2**20),
        name="assemble",
    )(flags, direct, mirror, diagonal, factor)


def moments_kernel(sums_ref, out_ref):
    total, squares, count = sums_ref[0:1, :], sums_ref[1:2, :], sums_ref[2:3, :]
    mean = total / count
    spread = jnp.maximum(squares - total * mean, 0.0) + squares * (1.0 / 128.0)
    largest = jnp.maximum(jnp.max(spread, axis=1, keepdims=True), 1e-30)
    scale = jnp.exp2(jnp.floor(0.5 * jnp.log2(16384.0 / largest)))
    out_ref[...] = jnp.zeros_like(out_ref)
    out_ref[0:1, :] = mean
    out_ref[1:2, :] = jnp.broadcast_to(scale, mean.shape)
    out_ref[2:3, :] = count


def moments(sums):
    return pl.pallas_call(
        moments_kernel,
        in_specs=[pl.BlockSpec(memory_space=pltpu.VMEM)],
        out_specs=pl.BlockSpec(memory_space=pltpu.VMEM),
        out_shape=jax.ShapeDtypeStruct(sums.shape, F32),
        name="moments",
    )(sums)


def center_kernel(chunk, chunks, x_ref, pack_ref, window_ref, out_ref, turned_ref):
    group = pl.program_id(0)
    rows = x_ref.shape[1]

    @pl.when(group == 0)
    def _():
        turned_ref[...] = pack_ref[...].T

    at = turned_ref[pl.ds(pl.multiple_of((group * chunks + chunk) * rows, 8), rows), :]
    centered = window_ref[...].astype(F32) * (x_ref[0].astype(F32) - at[:, 0:1])
    out_ref[0] = (centered.astype(BF16).astype(F32) * at[:, 1:2]).astype(BF16)


def center(x, pack, window, chunk, chunks):
    groups, rows, depth = x.shape
    return pl.pallas_call(
        functools.partial(center_kernel, chunk, chunks),
        grid=(groups,),
        in_specs=[
            pl.BlockSpec((1, rows, depth), lambda i: (i, 0, 0)),
            pl.BlockSpec(pack.shape, lambda i: (0, 0)),
            pl.BlockSpec((1, depth), lambda i: (0, 0)),
        ],
        out_specs=pl.BlockSpec((1, rows, depth), lambda i: (i, 0, 0)),
        out_shape=jax.ShapeDtypeStruct(x.shape, BF16),
        scratch_shapes=[pltpu.VMEM((pack.shape[1], 8), F32)],
        compiler_params=pltpu.CompilerParams(vmem_limit_bytes=16 * 2**20),
        cost_estimate=pl.CostEstimate(flops=0, bytes_accessed=0, transcendentals=0),
        name="center",
    )(x, pack, window)


def after(x, *gates):
    return lax.optimization_barrier((x,) + gates)[0] if gates else x


def solution(mesh):
    n_f, n_c = mesh.shape["frame"], mesh.shape["coord"]
    m = n_f // n_c
    low = m.bit_length() - 1
    high = n_c.bit_length() - 1
    n_pairs = n_c // 2

    def swap(x, axis, bit):
        return lax.ppermute(x, axis, [(i, i ^ bit) for i in range(mesh.shape[axis])])

    def on_device(frames, b_values, b_cols, frame_window):
        f, c = lax.axis_index("frame"), lax.axis_index("coord")
        coords, sums = project(frames, b_values, b_cols, frame_window)
        width, depth = coords.shape
        rows = width // m // CHUNKS
        raw = coords.reshape(m, CHUNKS, rows, depth)
        raw_far = {(d, 0): swap(raw[:, 0], "coord", d) for d in range(2, n_c, 2)}
        for j in range(n_f.bit_length() - 1):
            sums = sums + swap(sums, "frame", 1 << j)
        pack = moments(sums)
        mean, scale, count = pack[0], pack[1, 0], pack[2, 0]
        weight = frame_window.astype(F32)

        def center_far(x, mean, scale):
            centered = (weight * (x.astype(F32) - mean[..., None])).astype(BF16)
            return (centered.astype(F32) * scale).astype(BF16)

        mine = center(
            coords.reshape(m * CHUNKS, rows, depth), pack, frame_window[None, :], 0, 1
        ).reshape(width, depth)
        flip = (f // m) ^ c
        a = f % m
        top = low - 1

        def direct_half(group, d):
            return (group >> top) ^ ((c ^ d) > c).astype(jnp.int32)

        own = mine.reshape(m, CHUNKS, rows, depth)
        panels = {}
        for k in range(CHUNKS):
            panels[0, k] = own[:, k]

        def near(k, *gates):
            panels[1, k] = swap(after(panels[0, k], *gates), "coord", 1)
            return panels[1, k]

        def far(k, *gates):
            for d in range(2, n_c, 2):
                mean_k = packs[d][0].reshape(m, CHUNKS, rows)[:, k]
                panels[d, k] = center_far(after(raw_far[d, k], *gates), mean_k, packs[d][1, 0])
            return [panels[d, k] for d in range(2, n_c, 2)]

        def far_near(k, *gates):
            for d in range(2, n_c, 2):
                panels[d + 1, k] = swap(after(panels[d, k], *gates), "coord", 1)
            return [panels[d + 1, k] for d in range(2, n_c, 2)]

        class Task:
            def __init__(self, k, pair, order):
                self.order, self.at = order, 0
                n = 1 << len(order)
                which, group, half = [], [], []
                for index in range(n):
                    e, delta = 0, 0
                    for pos, what in enumerate(order):
                        bit = (index >> (len(order) - 1 - pos)) & 1
                        if what == "d":
                            delta = bit
                        else:
                            e |= bit << what
                    which.append((flip & 1) ^ delta)
                    group.append(e ^ a)
                    half.append(direct_half(group[-1], 2 * pair + which[-1]))
                both = gram(
                    jnp.stack(which),
                    jnp.stack(group),
                    jnp.stack(half),
                    panels[2 * pair, k],
                    panels[2 * pair + 1, k],
                    mine,
                )
                self.send = both[n // 2 :].astype(F16)
                self.keep = both[: n // 2]

            def step(self, *gates):
                what = self.order[self.at]
                if self.at:
                    half = self.keep.shape[0] // 2
                    self.send, self.keep = self.keep[half:].astype(F16), self.keep[:half]
                got = swap(after(self.send, *gates), "frame", m if what == "d" else 1 << what)
                self.keep = self.keep + got.astype(F32)
                self.at += 1
                return got

            def low_steps(self, *gates):
                for _ in range(low):
                    got = self.step(*gates)
                return got

        def tasks(k, far_pairs, order):
            return [Task(k, pair, order) for pair in (range(1, n_pairs) if far_pairs else range(1))]

        def low_steps(group, *gates):
            return [t.low_steps(*gates) for t in group]

        def d_step(group, *gates):
            return [t.step(*gates) for t in group]

        done = {}

        def top_steps(k, *gates):
            parts = [t.keep[0] for t in held[k, 0] + held[k, 1]]
            last = None
            for j in range(1, high):
                pick = ((flip >> j) & 1) == 1
                after_step = []
                for l, h in zip(parts[0::2], parts[1::2]):
                    last = swap(after(jnp.where(pick, l, h).astype(F16), *gates), "frame", m << j)
                    after_step.append(jnp.where(pick, h, l) + last.astype(F32))
                parts = after_step
            done[k] = parts[0]
            return last

        def directed(x, pairs, *gates):
            return lax.ppermute(after(x, *gates), ("frame", "coord"), pairs)

        class Diagonal:
            def __init__(self):
                group = [e ^ a for e in range(m)]
                whole = mine.reshape(m, CHUNKS * rows, depth)
                half = [(g >> top) ^ 1 for g in group]
                zero = jnp.zeros((m,), jnp.int32)
                both = gram(zero, jnp.stack(group), jnp.stack(half), whole, whole, mine)
                self.keep, self.send = both[: m // 2], both[m // 2 :].astype(F16)

            def low_steps(self, *gates):
                for j in reversed(range(low)):
                    if j < top:
                        half = self.keep.shape[0] // 2
                        self.keep, self.send = self.keep[:half], self.keep[half:].astype(F16)
                    got = swap(after(self.send, *gates), "frame", 1 << j)
                    self.keep = self.keep + got.astype(F32)
                return [got]

            def panel_step(self, j, *gates):
                pairs = []
                for g in range(n_f):
                    for d in range(n_c):
                        if (((g // m) ^ d) & ((2 << j) - 1)) == 1 << j:
                            pairs.append((g * n_c + d, (g ^ (m << j)) * n_c + d))
                got = directed(self.keep.astype(F16), pairs, *gates)
                self.keep = self.keep + got.astype(F32)
                return [got]

        mirrored = {}

        def mirror(k, *gates):
            group_width = CHUNKS * rows
            for i in range(m // 2):
                pairs = []
                for r in range(n_c):
                    for g in range(m):
                        for d in range(n_c):
                            if r != d:
                                there = (((g >> top) ^ (r > d)) << top) | ((g & (m // 2 - 1)) ^ i)
                                pairs.append(((r * m + g) * n_c + d, (d * m + there) * n_c + r))
                begin = ((a & (m // 2 - 1)) ^ i) * group_width
                block = done[k] if m == 2 else lax.dynamic_slice_in_dim(done[k], begin, group_width, 1)
                mirrored[i, k] = directed(block.astype(F16), pairs, *gates)
            return [mirrored[i, k] for i in range(m // 2)]

        low_first = list(reversed(range(low))) + ["d"]
        d_first = ["d"] + list(reversed(range(low)))
        held = {}

        def sends(k, far_pairs):
            return [t.send for t in held[k, far_pairs]]

        diagonal = Diagonal()
        ye = diagonal.low_steps()
        first = diagonal.send
        packs = {0: pack, 1: swap(after(pack, first), "coord", 1)}
        for d in range(2, n_c, 2):
            packs[d] = swap(after(pack, first), "coord", d)
            for k in range(1, CHUNKS):
                raw_far[d, k] = swap(after(raw[:, k], pack), "coord", d)
            packs[d + 1] = swap(packs[d], "coord", 1)

        row_scale = pack[:, :128]
        for d in range(1, n_c):
            row_scale = jnp.where(flip == d, packs[d][:, :128], row_scale)
        row_scale = row_scale[1:2]
        factor = 1.0 / (row_scale * scale * (count - 1.0))

        near(0, first)
        near(1, first)
        held[0, 0] = tasks(0, False, d_first)
        z00 = d_step(held[0, 0], diagonal.send)
        held[1, 0] = tasks(1, False, low_first)
        y10 = low_steps(held[1, 0], *sends(0, 0))
        far(0)
        far_near(0)
        held[0, 1] = tasks(0, True, d_first)

        ze = diagonal.panel_step(0, *(ye + sends(0, 0) + sends(1, 0)))
        b0 = ye + z00 + sends(1, 0) + sends(0, 1)
        y00 = low_steps(held[0, 0], *b0)
        z01 = d_step(held[0, 1], *b0)
        for j in range(1, high):
            te = diagonal.panel_step(j, *(ze + b0))
        far(1, *b0)
        far_near(1)
        held[1, 1] = tasks(1, True, low_first)

        b1 = z01 + y10 + y00 + [factor]
        y01 = low_steps(held[0, 1], *b1)
        y11 = low_steps(held[1, 1], *(y01 + te))
        z10 = d_step(held[1, 0], *y01)

        t0 = top_steps(0, *y01)

        b3 = y11 + [t0] + z10
        z11 = d_step(held[1, 1], *b3)
        m0 = mirror(0)
        top_steps(1, *(z11 + m0))
        mirror(1)

        direct = jnp.concatenate([done[k] for k in range(CHUNKS)])
        blocks = jnp.stack(
            [jnp.concatenate([mirrored[i, k] for k in range(CHUNKS)]).astype(F32) for i in range(m // 2)]
        )
        flags = jnp.stack(
            [direct_half(a, flip), (flip == 0).astype(jnp.int32), a & (m // 2 - 1)]
        )
        covariance = assemble(
            flags, direct, blocks, diagonal.keep[0], factor
        )
        return count, mean, covariance

    return jax.shard_map(
        on_device,
        mesh=mesh,
        in_specs=(P("frame", None), P("coord", None), P("coord", None), P("frame")),
        out_specs=(P(), P("coord"), P("frame", "coord")),
        check_vma=False,
    )
```

```python
import functools

import jax
import jax.numpy as jnp
from jax import lax
from jax.experimental import pallas as pl
from jax.experimental.pallas import tpu as pltpu
from jax.sharding import PartitionSpec as P

BLOCK = 64
CHUNKS = 2
F32, F16, BF16 = jnp.float32, jnp.float16, jnp.bfloat16


def project_kernel(cols_ref, frames_ref, values_ref, window_ref, out_ref, sums_ref, dense_ref):
    row_blocks, nonzero = cols_ref.shape

    @pl.when(pl.program_id(0) == 0)
    def _():
        dense_ref[...] = jnp.zeros_like(dense_ref)
        sums_ref[...] = jnp.zeros_like(sums_ref)
        for r in range(0, row_blocks, 2):
            block = values_ref[r * BLOCK : (r + 2) * BLOCK, :].T
            for h in range(2):
                for k in range(nonzero):
                    start = pl.multiple_of(cols_ref[r + h, k] * BLOCK, BLOCK)
                    dense_ref[pl.ds(start, BLOCK), (r + h) * BLOCK : (r + h + 1) * BLOCK] = block[
                        k * BLOCK : (k + 1) * BLOCK, h * BLOCK : (h + 1) * BLOCK
                    ]

    product = jnp.dot(frames_ref[...], dense_ref[...], preferred_element_type=F32)
    coords = product.astype(BF16)
    out_ref[...] = coords.T
    window = window_ref[...].astype(F32)
    weight = jnp.broadcast_to(window, (8, window.shape[1])).astype(BF16)
    sums_ref[0:1, :] += jnp.dot(weight, coords, preferred_element_type=F32)[0:1]
    sums_ref[1:2, :] += jnp.dot(weight, coords * coords, preferred_element_type=F32)[0:1]
    count = jnp.sum(window, axis=1, keepdims=True)
    sums_ref[2:3, :] += jnp.broadcast_to(count, (1, coords.shape[1]))


def project(frames, values, cols, window):
    rows, cart = frames.shape
    width = values.shape[0]
    tile = min(256, rows)
    return pl.pallas_call(
        project_kernel,
        grid=(rows // tile,),
        in_specs=[
            pl.BlockSpec(memory_space=pltpu.SMEM),
            pl.BlockSpec((tile, cart), lambda i: (i, 0)),
            pl.BlockSpec(values.shape, lambda i: (0, 0)),
            pl.BlockSpec((1, tile), lambda i: (0, i)),
        ],
        out_specs=[
            pl.BlockSpec((width, tile), lambda i: (0, i)),
            pl.BlockSpec((8, width), lambda i: (0, 0)),
        ],
        out_shape=[
            jax.ShapeDtypeStruct((width, rows), BF16),
            jax.ShapeDtypeStruct((8, width), F32),
        ],
        scratch_shapes=[pltpu.VMEM((cart, width), BF16)],
        compiler_params=pltpu.CompilerParams(vmem_limit_bytes=48 * 2**20),
        cost_estimate=pl.CostEstimate(
            flops=2 * rows * cart * width, bytes_accessed=2 * rows * (cart + width), transcendentals=0
        ),
        name="project",
    )(cols, frames, values, window[None, :])


def gram_kernel(which_ref, group_ref, half_ref, first_ref, second_ref, mine_ref, out_ref):
    part = pl.program_id(0)

    def write(left):
        out_ref[0] = lax.dot_general(
            left, mine_ref[...], (((1,), (1,)), ((), ())), preferred_element_type=F32
        )

    @pl.when(which_ref[part] == 0)
    def _():
        write(first_ref[0])

    @pl.when(which_ref[part] != 0)
    def _():
        write(second_ref[0])


def gram(which, group, half, first, second, mine):
    n = which.shape[0]
    _, rows, depth = first.shape
    width = mine.shape[0] // 2
    return pl.pallas_call(
        gram_kernel,
        grid_spec=pltpu.PrefetchScalarGridSpec(
            num_scalar_prefetch=3,
            grid=(n,),
            in_specs=[
                pl.BlockSpec((1, rows, depth), lambda i, which, group, half: (group[i], 0, 0)),
                pl.BlockSpec((1, rows, depth), lambda i, which, group, half: (group[i], 0, 0)),
                pl.BlockSpec((width, depth), lambda i, which, group, half: (half[i], 0)),
            ],
            out_specs=pl.BlockSpec((1, rows, width), lambda i, which, group, half: (i, 0, 0)),
        ),
        out_shape=jax.ShapeDtypeStruct((n, rows, width), F32),
        compiler_params=pltpu.CompilerParams(vmem_limit_bytes=24 * 2**20),
        cost_estimate=pl.CostEstimate(flops=0, bytes_accessed=0, transcendentals=0),
        name="gram",
    )(which, group, half, first, second, mine)


def assemble_kernel(flags_ref, direct_ref, mirror_ref, diagonal_ref, factor_ref, out_ref):
    groups, _, group_width = mirror_ref.shape
    half_width = direct_ref.shape[1]
    factor = factor_ref[0:1, 0:1]
    second = flags_ref[0] != 0

    def write(begin, value):
        out_ref[:, begin : begin + value.shape[1]] = value * factor

    def write_other(begin):
        @pl.when(flags_ref[1] != 0)
        def _():
            write(begin, diagonal_ref[...])

        @pl.when(flags_ref[1] == 0)
        def _():
            for pos in range(groups):
                write(begin + pos * group_width, mirror_ref[pos ^ flags_ref[2]].T)

    @pl.when(second)
    def _():
        write(half_width, direct_ref[...])
        write_other(0)

    @pl.when(jnp.logical_not(second))
    def _():
        write(0, direct_ref[...])
        write_other(half_width)


def assemble(flags, direct, mirror, diagonal, factor):
    rows, half_width = direct.shape
    return pl.pallas_call(
        assemble_kernel,
        in_specs=[pl.BlockSpec(memory_space=pltpu.SMEM)]
        + [pl.BlockSpec(memory_space=pltpu.VMEM)] * 4,
        out_specs=pl.BlockSpec(memory_space=pltpu.VMEM),
        out_shape=jax.ShapeDtypeStruct((rows, 2 * half_width), F32),
        compiler_params=pltpu.CompilerParams(vmem_limit_bytes=32 * 2**20),
        name="assemble",
    )(flags, direct, mirror, diagonal, factor)


def moments_kernel(sums_ref, out_ref):
    total, squares, count = sums_ref[0:1, :], sums_ref[1:2, :], sums_ref[2:3, :]
    mean = total / count
    spread = jnp.maximum(squares - total * mean, 0.0) + squares * (1.0 / 128.0)
    largest = jnp.maximum(jnp.max(spread, axis=1, keepdims=True), 1e-30)
    scale = jnp.exp2(jnp.floor(0.5 * jnp.log2(16384.0 / largest)))
    out_ref[...] = jnp.zeros_like(out_ref)
    out_ref[0:1, :] = mean
    out_ref[1:2, :] = jnp.broadcast_to(scale, mean.shape)
    out_ref[2:3, :] = count


def moments(sums):
    return pl.pallas_call(
        moments_kernel,
        in_specs=[pl.BlockSpec(memory_space=pltpu.VMEM)],
        out_specs=pl.BlockSpec(memory_space=pltpu.VMEM),
        out_shape=jax.ShapeDtypeStruct(sums.shape, F32),
        name="moments",
    )(sums)


def center_kernel(chunk, chunks, x_ref, pack_ref, window_ref, out_ref, turned_ref):
    group = pl.program_id(0)
    rows = x_ref.shape[1]

    @pl.when(group == 0)
    def _():
        turned_ref[...] = pack_ref[...].T

    at = turned_ref[pl.ds(pl.multiple_of((group * chunks + chunk) * rows, 8), rows), :]
    centered = window_ref[...].astype(F32) * (x_ref[0].astype(F32) - at[:, 0:1])
    out_ref[0] = (centered.astype(BF16).astype(F32) * at[:, 1:2]).astype(BF16)


def center(x, pack, window, chunk, chunks):
    groups, rows, depth = x.shape
    return pl.pallas_call(
        functools.partial(center_kernel, chunk, chunks),
        grid=(groups,),
        in_specs=[
            pl.BlockSpec((1, rows, depth), lambda i: (i, 0, 0)),
            pl.BlockSpec(pack.shape, lambda i: (0, 0)),
            pl.BlockSpec((1, depth), lambda i: (0, 0)),
        ],
        out_specs=pl.BlockSpec((1, rows, depth), lambda i: (i, 0, 0)),
        out_shape=jax.ShapeDtypeStruct(x.shape, BF16),
        scratch_shapes=[pltpu.VMEM((pack.shape[1], 8), F32)],
        compiler_params=pltpu.CompilerParams(vmem_limit_bytes=16 * 2**20),
        cost_estimate=pl.CostEstimate(flops=0, bytes_accessed=0, transcendentals=0),
        name="center",
    )(x, pack, window)


def after(x, *gates):
    return lax.optimization_barrier((x,) + gates)[0] if gates else x


def solution(mesh):
    n_f, n_c = mesh.shape["frame"], mesh.shape["coord"]
    m = n_f // n_c
    low = m.bit_length() - 1
    high = n_c.bit_length() - 1
    n_pairs = n_c // 2

    def swap(x, axis, bit):
        return lax.ppermute(x, axis, [(i, i ^ bit) for i in range(mesh.shape[axis])])

    def on_device(frames, b_values, b_cols, frame_window):
        f, c = lax.axis_index("frame"), lax.axis_index("coord")
        coords, sums = project(frames, b_values, b_cols, frame_window)
        width, depth = coords.shape
        rows = width // m // CHUNKS
        raw = coords.reshape(m, CHUNKS, rows, depth)
        raw_far = {(d, 0): swap(raw[:, 0], "coord", d) for d in range(2, n_c, 2)}
        for j in range(n_f.bit_length() - 1):
            sums = sums + swap(sums, "frame", 1 << j)
        pack = moments(sums)
        mean, scale, count = pack[0], pack[1, 0], pack[2, 0]
        weight = frame_window.astype(F32)

        def center_far(x, mean, scale):
            centered = (weight * (x.astype(F32) - mean[..., None])).astype(BF16)
            return (centered.astype(F32) * scale).astype(BF16)

        mine = center(
            coords.reshape(m * CHUNKS, rows, depth), pack, frame_window[None, :], 0, 1
        ).reshape(width, depth)
        flip = (f // m) ^ c
        a = f % m
        top = low - 1

        def direct_half(group, d):
            return (group >> top) ^ ((c ^ d) > c).astype(jnp.int32)

        own = mine.reshape(m, CHUNKS, rows, depth)
        panels = {}
        for k in range(CHUNKS):
            panels[0, k] = own[:, k]

        def near(k, *gates):
            panels[1, k] = swap(after(panels[0, k], *gates), "coord", 1)
            return panels[1, k]

        def far(k, *gates):
            for d in range(2, n_c, 2):
                mean_k = packs[d][0].reshape(m, CHUNKS, rows)[:, k]
                panels[d, k] = center_far(after(raw_far[d, k], *gates), mean_k, packs[d][1, 0])
            return [panels[d, k] for d in range(2, n_c, 2)]

        def far_near(k, *gates):
            for d in range(2, n_c, 2):
                panels[d + 1, k] = swap(after(panels[d, k], *gates), "coord", 1)
            return [panels[d + 1, k] for d in range(2, n_c, 2)]

        class Task:
            def __init__(self, k, pair, order):
                self.order, self.at = order, 0
                n = 1 << len(order)
                which, group, half = [], [], []
                for index in range(n):
                    e, delta = 0, 0
                    for pos, what in enumerate(order):
                        bit = (index >> (len(order) - 1 - pos)) & 1
                        if what == "d":
                            delta = bit
                        else:
                            e |= bit << what
                    which.append((flip & 1) ^ delta)
                    group.append(e ^ a)
                    half.append(direct_half(group[-1], 2 * pair + which[-1]))
                both = gram(
                    jnp.stack(which),
                    jnp.stack(group),
                    jnp.stack(half),
                    panels[2 * pair, k],
                    panels[2 * pair + 1, k],
                    mine,
                )
                self.send = both[n // 2 :].astype(F16)
                self.keep = both[: n // 2]

            def step(self, *gates):
                what = self.order[self.at]
                if self.at:
                    half = self.keep.shape[0] // 2
                    self.send, self.keep = self.keep[half:].astype(F16), self.keep[:half]
                got = swap(after(self.send, *gates), "frame", m if what == "d" else 1 << what)
                self.keep = self.keep + got.astype(F32)
                self.at += 1
                return got

            def low_steps(self, *gates):
                for _ in range(low):
                    got = self.step(*gates)
                return got

        def tasks(k, far_pairs, order):
            return [Task(k, pair, order) for pair in (range(1, n_pairs) if far_pairs else range(1))]

        def low_steps(group, *gates):
            return [t.low_steps(*gates) for t in group]

        def d_step(group, *gates):
            return [t.step(*gates) for t in group]

        done = {}

        def top_steps(k, *gates):
            parts = [t.keep[0] for t in held[k, 0] + held[k, 1]]
            last = None
            for j in range(1, high):
                pick = ((flip >> j) & 1) == 1
                after_step = []
                for l, h in zip(parts[0::2], parts[1::2]):
                    last = swap(after(jnp.where(pick, l, h).astype(F16), *gates), "frame", m << j)
                    after_step.append(jnp.where(pick, h, l) + last.astype(F32))
                parts = after_step
            done[k] = parts[0]
            return last

        def directed(x, pairs, *gates):
            return lax.ppermute(after(x, *gates), ("frame", "coord"), pairs)

        class Diagonal:
            def __init__(self):
                group = [e ^ a for e in range(m)]
                whole = mine.reshape(m, CHUNKS * rows, depth)
                half = [(g >> top) ^ 1 for g in group]
                zero = jnp.zeros((m,), jnp.int32)
                both = gram(zero, jnp.stack(group), jnp.stack(half), whole, whole, mine)
                self.keep, self.send = both[: m // 2], both[m // 2 :].astype(F16)

            def low_steps(self, *gates):
                for j in reversed(range(low)):
                    if j < top:
                        half = self.keep.shape[0] // 2
                        self.keep, self.send = self.keep[:half], self.keep[half:].astype(F16)
                    got = swap(after(self.send, *gates), "frame", 1 << j)
                    self.keep = self.keep + got.astype(F32)
                return [got]

            def panel_step(self, j, *gates):
                pairs = []
                for g in range(n_f):
                    for d in range(n_c):
                        if (((g // m) ^ d) & ((2 << j) - 1)) == 1 << j:
                            pairs.append((g * n_c + d, (g ^ (m << j)) * n_c + d))
                got = directed(self.keep.astype(F16), pairs, *gates)
                self.keep = self.keep + got.astype(F32)
                return [got]

        mirrored = {}

        def mirror(k, *gates):
            group_width = CHUNKS * rows
            for i in range(m // 2):
                pairs = []
                for r in range(n_c):
                    for g in range(m):
                        for d in range(n_c):
                            if r != d:
                                there = (((g >> top) ^ (r > d)) << top) | ((g & (m // 2 - 1)) ^ i)
                                pairs.append(((r * m + g) * n_c + d, (d * m + there) * n_c + r))
                begin = ((a & (m // 2 - 1)) ^ i) * group_width
                block = done[k] if m == 2 else lax.dynamic_slice_in_dim(done[k], begin, group_width, 1)
                mirrored[i, k] = directed(block.astype(F16), pairs, *gates)
            return [mirrored[i, k] for i in range(m // 2)]

        low_first = list(reversed(range(low))) + ["d"]
        d_first = ["d"] + list(reversed(range(low)))
        held = {}

        def sends(k, far_pairs):
            return [t.send for t in held[k, far_pairs]]

        diagonal = Diagonal()
        ye = diagonal.low_steps()
        first = diagonal.send
        packs = {0: pack, 1: swap(after(pack, first), "coord", 1)}
        for d in range(2, n_c, 2):
            packs[d] = swap(after(pack, first), "coord", d)
            for k in range(1, CHUNKS):
                raw_far[d, k] = swap(after(raw[:, k], pack), "coord", d)
            packs[d + 1] = swap(packs[d], "coord", 1)

        row_scale = pack[:, :128]
        for d in range(1, n_c):
            row_scale = jnp.where(flip == d, packs[d][:, :128], row_scale)
        row_scale = row_scale[1:2]
        factor = 1.0 / (row_scale * scale * (count - 1.0))

        near(0, first)
        near(1, first)
        held[0, 0] = tasks(0, False, d_first)
        z00 = d_step(held[0, 0], diagonal.send)
        held[1, 0] = tasks(1, False, low_first)
        y10 = low_steps(held[1, 0], *sends(0, 0))
        far(0)
        far_near(0)
        held[0, 1] = tasks(0, True, d_first)

        ze = diagonal.panel_step(0, *(ye + sends(0, 0) + sends(1, 0)))
        b0 = ye + z00 + sends(1, 0) + sends(0, 1)
        y00 = low_steps(held[0, 0], *b0)
        z01 = d_step(held[0, 1], *b0)
        for j in range(1, high):
            te = diagonal.panel_step(j, *(ze + b0))
        far(1, *b0)
        far_near(1)
        held[1, 1] = tasks(1, True, low_first)

        b1 = z01 + y10 + y00 + [factor]
        y01 = low_steps(held[0, 1], *b1)
        y11 = low_steps(held[1, 1], *(y01 + te))
        z10 = d_step(held[1, 0], *y01)

        t0 = top_steps(0, *y01)

        b3 = y11 + [t0] + z10
        z11 = d_step(held[1, 1], *b3)
        m0 = mirror(0)
        top_steps(1, *z11)
        mirror(1)

        direct = jnp.concatenate([done[k] for k in range(CHUNKS)])
        blocks = jnp.stack(
            [jnp.concatenate([mirrored[i, k] for k in range(CHUNKS)]).astype(F32) for i in range(m // 2)]
        )
        flags = jnp.stack(
            [direct_half(a, flip), (flip == 0).astype(jnp.int32), a & (m // 2 - 1)]
        )
        covariance = assemble(
            flags, direct, blocks, diagonal.keep[0], factor
        )
        return count, mean, covariance

    return jax.shard_map(
        on_device,
        mesh=mesh,
        in_specs=(P("frame", None), P("coord", None), P("coord", None), P("frame")),
        out_specs=(P(), P("coord"), P("frame", "coord")),
        check_vma=False,
    )
```
